32 devices in a mesh: bx: 4 (over z), by: 8 (over y, x, core).
Axes of the slice: x: 2, y: 2, z: 4, core: 2. Of those that a mesh axis runs over, the one named last changes fastest.
Arguments:
- right_side: float32 [16, 64, 256, 128], P(None, 'bx', 'by'), may hold values from -14 to 14
- conductivity: float32 [64, 256, 128], P('bx', 'by'), may hold values from 0.5 to 1
Outputs:
- solution_field: float32 [16, 64, 256, 128], P(None, 'bx', 'by')
- residual: float32 [16, 64, 256, 128], P(None, 'bx', 'by')
The draws below stay inside these ranges and needn't reach their ends.
All inputs are finite; a program needn't handle non-finite values.
Results may differ from the reference program's by a relative error of at most 0.023.
Values sent between devices are 32-bit elements; how exact they have to be, the bound alone decides.
A program may use at most 192 MiB of HBM per device.

```python
import math
import jax
import jax.numpy as jnp
import numpy as np
from jax import lax

S = 16
STEPS = 4
CX = 16
CY = 32
CZ = 128
NX = 64
NY = 256


def front_offset(key):
    key_x, key_y, key_sign = jax.random.split(key, 3)
    brick_x = jax.random.randint(key_x, (S, 1, 1, 1), 0, NX // CX)
    brick_y = jax.random.randint(key_y, (S, 1, 1, 1), 0, NY // CY)
    signs = jnp.where(jax.random.randint(key_sign, (S, 1, 1, 1), 0, 2) == 1, 1.0, -1.0)
    cell_x = jnp.arange(NX, dtype=jnp.int32).reshape(1, NX, 1, 1) // CX
    cell_y = jnp.arange(NY, dtype=jnp.int32).reshape(1, 1, NY, 1) // CY
    inside = jnp.logical_and(cell_x == brick_x, cell_y == brick_y)
    return jnp.where(inside, 8.0, 0.0) * signs


def draw_right_side(key, part):
    key = jax.random.fold_in(key, 11)
    key_front, key = jax.random.split(key)
    shape = (S, NX, NY, CZ)
    offset = front_offset(key_front)
    return jnp.clip(jax.random.normal(key, shape, jnp.float32), -6.0, 6.0) + offset


def steps_of(rng, extent, pieces, least, largest):
    def one(axis_at, blocks):
        steps = jax.random.uniform(jax.random.fold_in(jax.random.fold_in(rng, 6), axis_at), (blocks,), jnp.float32, least / len(pieces), largest / len(pieces))
        return jnp.repeat(jnp.exp(steps), extent[axis_at] // blocks).reshape((-1,) + (1,) * (len(extent) - axis_at - 1))

    level = one(*pieces[0])
    for cut in pieces[1:]:
        level = level * one(*cut)
    return level


def setup_inputs(seed: int = 0) -> dict:
    key_of = jax.random.split(jax.random.key(seed), 3)
    return {
        "right_side": draw_right_side(jax.random.fold_in(key_of[2], 71), 0),
        "conductivity": jnp.clip(jnp.exp(math.log(1.0) - 0.6931472 * jax.random.uniform(key_of[1], (NX, NY, CZ), jnp.float32) ** steps_of(key_of[1], (NX, NY, CZ), ((0, 4), (1, 8)), -0.2, 0.2)), 0.5, 1.0),
    }


spectrum_center = 7.0
spectrum_radius = 6.0
face_offsets = ((1, 0, 0), (-1, 0, 0), (0, 1, 0), (0, -1, 0), (0, 0, 1), (0, 0, -1))

def neighbour(array, off_x, off_y, off_z):
    size_x, size_y, size_z = array.shape[-3:]
    return array[..., 1 + off_x:size_x - 1 + off_x, 1 + off_y:size_y - 1 + off_y, 1 + off_z:size_z - 1 + off_z]

def apply_shifted(field_pad, coeff_pad):
    coeff_z = jnp.pad(coeff_pad, ((0, 0), (0, 0), (1, 1)))
    field_z = jnp.pad(field_pad, ((0, 0), (0, 0), (0, 0), (1, 1)))
    center_k = neighbour(coeff_z, 0, 0, 0)
    center_v = neighbour(field_z, 0, 0, 0)
    total = center_v
    for offset in face_offsets:
        other_k = neighbour(coeff_z, *offset)
        denom = center_k + other_k
        inside = denom > 0.0
        face = jnp.where(inside, 2.0 * center_k * other_k / jnp.where(inside, denom, 1.0), 0.0)
        total = total + face * (center_v - neighbour(field_z, *offset))
    return (total - spectrum_center * center_v) / spectrum_radius

def cheb_table():
    table = np.zeros((STEPS + 1, STEPS))
    table[0, 0] = 7.0
    table[1, 0] = 6.0
    for power in range(1, STEPS):
        table[power, power] = 7.0
        table[power - 1, power] = 3.0
        table[power + 1, power] = 3.0
    return np.kron(table, np.eye(S))

def solve_normal(normal, load):
    highest = lax.Precision.HIGHEST
    order = normal.shape[0]
    places = jnp.arange(order, dtype=jnp.int32)

    def chol_step(j, factor):
        pick = (places == j).astype(normal.dtype)
        column = jnp.dot(normal, pick, precision=highest) - jnp.dot(factor, jnp.dot(pick, factor, precision=highest), precision=highest)
        pivot = jnp.sqrt(jnp.dot(pick, column, precision=highest))
        column = jnp.where(places >= j, column / pivot, 0.0)
        return factor + column[:, None] * pick[None, :]
    factor = lax.fori_loop(0, order, chol_step, jnp.zeros_like(normal))

    def forward_step(j, solved):
        pick = (places == j).astype(normal.dtype)
        row = jnp.dot(pick, factor, precision=highest)
        value = (jnp.dot(pick, load, precision=highest) - jnp.dot(row, solved, precision=highest)) / jnp.dot(row, pick, precision=highest)
        return solved + pick[:, None] * value[None, :]
    inner = lax.fori_loop(0, order, forward_step, jnp.zeros_like(load))

    def backward_step(i, solved):
        j = order - 1 - i
        pick = (places == j).astype(normal.dtype)
        row = jnp.dot(factor, pick, precision=highest)
        value = (jnp.dot(pick, inner, precision=highest) - jnp.dot(row, solved, precision=highest)) / jnp.dot(row, pick, precision=highest)
        return solved + pick[:, None] * value[None, :]
    return lax.fori_loop(0, order, backward_step, jnp.zeros_like(load))

def small_solve(gram):
    table = jnp.asarray(cheb_table(), gram.dtype)
    highest = lax.Precision.HIGHEST
    normal = jnp.dot(table.T, jnp.dot(gram, table, precision=highest), precision=highest)
    load = jnp.dot(table.T, gram[:, :S], precision=highest)
    coeffs = solve_normal(normal, load)
    return (coeffs, jnp.dot(table, coeffs, precision=highest))

def reference(right_side, conductivity):
    highest = lax.Precision.HIGHEST
    coeff_pad = jnp.pad(conductivity, ((1, 1), (1, 1), (0, 0)))

    def power_step(field):
        return apply_shifted(jnp.pad(field, ((0, 0), (1, 1), (1, 1), (0, 0))), coeff_pad)
    blocks = [right_side, power_step(right_side)]
    for power in range(1, STEPS):
        blocks.append(2.0 * power_step(blocks[power]) - blocks[power - 1])
    matrix = jnp.stack(blocks).reshape(S * (STEPS + 1), -1)
    gram = jnp.dot(matrix, matrix.T, precision=highest)
    coeffs, combined = small_solve(gram)
    solution_field = jnp.dot(coeffs.T, matrix[:S * STEPS], precision=highest).reshape(right_side.shape)
    residual = right_side - jnp.dot(combined.T, matrix, precision=highest).reshape(right_side.shape)
    return (solution_field, residual)
```

```python
import functools

import jax
import jax.numpy as jnp
import numpy as np
from jax import lax
from jax.experimental import pallas as pl
from jax.experimental.pallas import tpu as pltpu
from jax.sharding import PartitionSpec as P

S = 16
STEPS = 4
MESH = pl.DeviceIdType.MESH


def cheb_small():
    table = np.zeros((STEPS + 1, STEPS))
    table[0, 0] = 7.0
    table[1, 0] = 6.0
    for power in range(1, STEPS):
        table[power, power] = 7.0
        table[power - 1, power] = 3.0
        table[power + 1, power] = 3.0
    return table


def split(a):
    hi = a.astype(jnp.bfloat16)
    lo = (a - hi.astype(jnp.float32)).astype(jnp.bfloat16)
    return hi, lo


def basis_kernel(
    nbx, nby, X, Y, rhs, k_ref, w_out, g_out,
    v, kp, cx, cy, czm, czp, cd, gl, r1, r2,
    in_sem, out_sem, k_send, k_recv, h_send, h_recv, a_send, a_recv, b_send, b_recv,
):
    bx, by = lax.axis_index("bx"), lax.axis_index("by")
    barrier = pltpu.get_barrier_semaphore()

    loads = [
        pltpu.make_async_copy(rhs.at[s], v.at[0, pl.ds(1, X), pl.ds(1, Y), s], in_sem.at[s])
        for s in range(S)
    ]
    for c in loads:
        c.start()
    for d in range(1, nbx):
        pl.semaphore_signal(barrier, inc=1, device_id=(lax.rem(bx + d, nbx), by), device_id_type=MESH)
    for d in range(1, nby):
        pl.semaphore_signal(barrier, inc=1, device_id=(bx, lax.rem(by + d, nby)), device_id_type=MESH)

    @pl.loop(0, X)
    def _(x):
        kp[x + 1, pl.ds(1, Y)] = k_ref[x]

    edges = (bx > 0, bx < nbx - 1, by > 0, by < nby - 1)

    def zero_side(side):
        if side < 2:
            at = 0 if side == 0 else X + 1
            kp[at] = jnp.zeros_like(kp[at])
            for j in range(STEPS):
                @pl.loop(0, Y + 2)
                def _(y):
                    v[j, at, y] = jnp.zeros((S, 128), jnp.float32)
        else:
            at = 0 if side == 2 else Y + 1
            @pl.loop(1, X + 1)
            def _(x):
                kp[x, at] = jnp.zeros((1, 128), jnp.float32)
                for j in range(STEPS):
                    v[j, x, at] = jnp.zeros((S, 128), jnp.float32)

    for side in range(4):
        pl.when(jnp.logical_not(edges[side]))(functools.partial(zero_side, side))
    pl.semaphore_wait(barrier, nbx - 1 + nby - 1)

    targets = ((bx - 1, by), (bx + 1, by), (bx, by - 1), (bx, by + 1))

    def face_copies(ref, send, recv, side):
        xs, ys = pl.ds(1, X), pl.ds(1, Y)
        src, dst = (
            (ref.at[1, ys], ref.at[X + 1, ys]),
            (ref.at[X, ys], ref.at[0, ys]),
            (ref.at[xs, 1], ref.at[xs, Y + 1]),
            (ref.at[xs, Y], ref.at[xs, 0]),
        )[side]
        return pltpu.make_async_remote_copy(
            src_ref=src, dst_ref=dst, send_sem=send.at[side], recv_sem=recv.at[side],
            device_id=targets[side], device_id_type=MESH,
        )

    def start_faces(ref, send, recv):
        for side in range(4):
            @pl.when(edges[side])
            def _(side=side):
                face_copies(ref, send, recv, side).start()

    def wait_recv(ref, send, recv):
        for side in range(4):
            @pl.when(edges[side])
            def _(side=side):
                face_copies(ref, send, recv, side ^ 1).wait_recv()

    def wait_send(ref, send, recv):
        for side in range(4):
            @pl.when(edges[side])
            def _(side=side):
                face_copies(ref, send, recv, side).wait_send()

    start_faces(kp, k_send, k_recv)
    for c in loads:
        c.wait()
    start_faces(v.at[0], h_send.at[0], h_recv.at[0])
    stores = [
        pltpu.make_async_copy(
            v.at[j, pl.ds(1, X), pl.ds(1, Y)], w_out.at[j], out_sem.at[j])
        for j in range(STEPS + 1)
    ]
    stores[0].start()
    wait_recv(kp, k_send, k_recv)

    def face(a, b):
        return (2.0 * a * b) / (a + b)

    third = -1.0 / 3.0

    def coeff_x(x, n, y0):
        cx[x, pl.ds(y0, n)] = third * face(kp[x, pl.ds(y0, n)], kp[x + 1, pl.ds(y0, n)])

    @pl.loop(0, X + 1)
    def _(x):
        coeff_x(x, Y, 1)

    lane = lax.broadcasted_iota(jnp.int32, (Y, 1, 128), 2)

    @pl.loop(1, X + 1)
    def _(x):
        k = kp[x, pl.ds(1, Y)]
        cy[x, pl.ds(1, Y)] = third * face(k, kp[x, pl.ds(2, Y)])
        cy[x, pl.ds(0, 1)] = third * face(kp[x, pl.ds(0, 1)], kp[x, pl.ds(1, 1)])
        up = jnp.where(lane == 127, 0.0, pltpu.roll(k, 127, 2))
        zp = third * face(k, up)
        zm = pltpu.roll(zp, 1, 2)
        czp[x, pl.ds(1, Y)] = zp
        czm[x, pl.ds(1, Y)] = zm
        total = cx[x - 1, pl.ds(1, Y)] + cx[x, pl.ds(1, Y)]
        total = total + cy[x, pl.ds(0, Y)] + cy[x, pl.ds(1, Y)] + zp + zm
        cd[x, pl.ds(1, Y)] = -total - 2.0

    def stencil(j, x, y0, n):
        ys = pl.ds(y0, n)
        c = v[j, x, ys]
        shape = c.shape

        def wide(a):
            return jnp.broadcast_to(a, shape)

        out = wide(cd[x, ys]) * c
        out = out + wide(czp[x, ys]) * pltpu.roll(c, 127, 2)
        out = out + wide(czm[x, ys]) * pltpu.roll(c, 1, 2)
        out = out + wide(cx[x - 1, ys]) * v[j, x - 1, ys]
        out = out + wide(cx[x, ys]) * v[j, x + 1, ys]
        out = out + wide(cy[x, pl.ds(y0 - 1, n)]) * v[j, x, pl.ds(y0 - 1, n)]
        out = out + wide(cy[x, ys]) * v[j, x, pl.ds(y0 + 1, n)]
        if j == 0:
            v[1, x, ys] = 0.5 * out
        else:
            v[j + 1, x, ys] = out - v[j - 1, x, ys]

    CH = 4

    def rows(j, x, lo, hi):
        count = (hi - lo) // CH

        @pl.loop(0, count)
        def _(i):
            stencil(j, x, lo + i * CH, CH)
        if (hi - lo) % CH:
            stencil(j, x, lo + count * CH, (hi - lo) % CH)

    def boundary(j):
        rows(j, 1, 1, Y + 1)
        rows(j, X, 1, Y + 1)

        @pl.loop(2, X)
        def _(x):
            stencil(j, x, 1, 1)
            stencil(j, x, Y, 1)

    def interior(j):
        @pl.loop(2, X)
        def _(x):
            rows(j, x, 2, Y)

    def flat(j, x):
        return jnp.concatenate([v[j, x, 1 + y] for y in range(Y)], axis=1)

    def gram(j):
        def body(x, total):
            hi, lo = split(flat(j, x))
            right = jnp.concatenate([hi, lo], axis=0)
            left = right
            if j > 0:
                phi, plo = split(flat(j - 1, x))
                left = jnp.concatenate([hi, lo, phi, plo], axis=0)
            return total + lax.dot_general(
                left, right, (((1,), (1,)), ((), ())), preferred_element_type=jnp.float32)

        n = 32 if j == 0 else 64
        total = lax.fori_loop(1, X + 1, body, jnp.zeros((n, 32), jnp.float32))
        cols = total[:, :16] + total[:, 16:]
        same = cols[0:16] + cols[16:32]
        gl[0:16, 16 * j:16 * j + 16] = same
        if j > 0:
            gl[16:32, 16 * j:16 * j + 16] = cols[32:48] + cols[48:64]

    gl[...] = jnp.zeros_like(gl)
    gram(0)
    for j in range(STEPS):
        wait_recv(v.at[j], h_send.at[j], h_recv.at[j])
        boundary(j)
        if j + 1 < STEPS:
            start_faces(v.at[j + 1], h_send.at[j + 1], h_recv.at[j + 1])
        interior(j)
        stores[j + 1].start()
        gram(j + 1)

    def spread(axis_at, n, own, src, slots, send, recv):
        copies = []
        for d in range(1, n):
            to = (lax.rem(bx + d, n), by) if axis_at == 0 else (bx, lax.rem(by + d, n))
            copies.append(pltpu.make_async_remote_copy(
                src_ref=src, dst_ref=slots.at[d], send_sem=send.at[d], recv_sem=recv.at[d],
                device_id=to, device_id_type=MESH))
        for c in copies:
            c.start()
        total = src[...]
        for d in range(1, n):
            copies[d - 1].wait_recv()
            total = total + slots[d]
        for c in copies:
            c.wait_send()
        return total

    gl2 = r1.at[0]
    gl2[...] = spread(0, nbx, bx, gl, r1, a_send, a_recv)
    g_out[...] = spread(1, nby, by, gl2, r2, b_send, b_recv)

    wait_send(kp, k_send, k_recv)
    for j in range(STEPS):
        wait_send(v.at[j], h_send.at[j], h_recv.at[j])
    for c in stores:
        c.wait()


def solve(g):
    table = cheb_small()
    same = [g[0:16, 16 * j:16 * j + 16] for j in range(STEPS + 1)]
    cross = [None] + [g[16:32, 16 * j:16 * j + 16] for j in range(1, STEPS + 1)]
    moment = [same[0], cross[1]]
    for k in range(1, STEPS + 1):
        moment.append(2.0 * same[k] - same[0])
        if k < STEPS:
            moment.append(2.0 * cross[k + 1] - cross[1])

    def weighted(weights):
        out = None
        for m, w in zip(moment, weights):
            if w != 0.0:
                out = w * m if out is None else out + w * m
        return out

    rows = []
    for i in range(STEPS):
        blocks = []
        for j in range(STEPS):
            weights = np.zeros(2 * STEPS + 1)
            for a in range(STEPS + 1):
                for b in range(STEPS + 1):
                    w = 0.5 * table[a, i] * table[b, j]
                    weights[a + b] += w
                    weights[abs(a - b)] += w
            blocks.append(weighted([float(w) for w in weights]))
        blocks.append(weighted([float(w) for w in table[:, i]] + [0.0] * STEPS))
        blocks.append(jnp.zeros((16, 48), jnp.float32))
        rows.append(jnp.concatenate(blocks, axis=1))
    a = jnp.concatenate(rows, axis=0)
    order = S * STEPS
    place = lax.broadcasted_iota(jnp.int32, (order, 128), 0)
    for p in range(order):
        col = jnp.broadcast_to(a[:, p:p + 1], (order, 128))
        row = jnp.broadcast_to(a[p:p + 1] / col[p:p + 1], (order, 128))
        a = jnp.where(place == p, row, a - col * row)
    coeffs = [a[16 * i:16 * i + 16, order:order + 16] for i in range(STEPS)]
    zero = jnp.zeros((16, 16), jnp.float32)
    eye = jnp.where(
        lax.broadcasted_iota(jnp.int32, (16, 16), 0) == lax.broadcasted_iota(jnp.int32, (16, 16), 1),
        1.0, 0.0)
    parts = []
    for r in range(STEPS + 1):
        rest = eye if r == 0 else zero
        for i in range(STEPS):
            if table[r, i] != 0.0:
                rest = rest - float(table[r, i]) * coeffs[i]
        first = coeffs[r] if r < STEPS else zero
        parts.append(jnp.concatenate([first, rest, jnp.zeros((16, 96), jnp.float32)], axis=1))
    c = jnp.concatenate(parts, axis=0)
    hi = c.astype(jnp.bfloat16).astype(jnp.float32)
    lo = c - hi
    return jnp.concatenate([hi, hi, lo, jnp.zeros((16, 128), jnp.float32)], axis=0)


def combine_kernel(Y, g_ref, w_ref, sol_ref, res_ref, c_ref):
    @pl.when(pl.program_id(0) == 0)
    def _():
        stacked = solve(g_ref[...])
        c_ref[...] = stacked.T[0:32].astype(jnp.bfloat16)

    CH = 8

    @pl.loop(0, Y // CH)
    def _(t):
        y0 = pl.multiple_of(t * CH, CH)
        cols = []
        for y in range(CH):
            his, los = [], []
            for j in range(STEPS + 1):
                hi, lo = split(w_ref[j, 0, y0 + y])
                his.append(hi)
                los.append(lo)
            cols.append(jnp.concatenate(
                his + los + his + [jnp.zeros((16, 128), jnp.bfloat16)], axis=0))
        right = jnp.concatenate(cols, axis=1)
        out = jnp.dot(c_ref[...], right, preferred_element_type=jnp.float32)
        out = jnp.stack([out[:, 128 * y:128 * y + 128] for y in range(CH)], axis=0)
        out = jnp.swapaxes(out, 0, 1)
        sol_ref[:, 0, pl.ds(y0, CH)] = out[0:16]
        res_ref[:, 0, pl.ds(y0, CH)] = out[16:32]


def shards(right_side, conductivity):
    nbx, nby = lax.axis_size("bx"), lax.axis_size("by")
    X, Y, Z = conductivity.shape
    f32 = jnp.float32
    dma = pltpu.SemaphoreType.DMA
    w, g = pl.pallas_call(
        functools.partial(basis_kernel, nbx, nby, X, Y),
        out_shape=(
            jax.ShapeDtypeStruct((STEPS + 1, X, Y, S, Z), f32),
            jax.ShapeDtypeStruct((32, 128), f32),
        ),
        in_specs=[pl.BlockSpec(memory_space=pl.ANY), pl.BlockSpec(memory_space=pltpu.VMEM)],
        out_specs=(pl.BlockSpec(memory_space=pl.ANY), pl.BlockSpec(memory_space=pltpu.VMEM)),
        scratch_shapes=[
            pltpu.VMEM((STEPS + 1, X + 2, Y + 2, S, Z), f32),
            pltpu.VMEM((X + 2, Y + 2, 1, Z), f32),
            pltpu.VMEM((X + 2, Y + 2, 1, Z), f32),
            pltpu.VMEM((X + 2, Y + 2, 1, Z), f32),
            pltpu.VMEM((X + 2, Y + 2, 1, Z), f32),
            pltpu.VMEM((X + 2, Y + 2, 1, Z), f32),
            pltpu.VMEM((X + 2, Y + 2, 1, Z), f32),
            pltpu.VMEM((32, 128), f32),
            pltpu.VMEM((nbx, 32, 128), f32),
            pltpu.VMEM((nby, 32, 128), f32),
            dma((S,)), dma((STEPS + 1,)), dma((4,)), dma((4,)),
            dma((STEPS, 4)), dma((STEPS, 4)),
            dma((nbx,)), dma((nbx,)), dma((nby,)), dma((nby,)),
        ],
        compiler_params=pltpu.CompilerParams(
            collective_id=0, has_side_effects=True, vmem_limit_bytes=56 * 1024 * 1024),
        name="basis",
    )(right_side, conductivity.reshape(X, Y, 1, Z))
    out = jax.ShapeDtypeStruct((S, X, Y, Z), f32)
    return pl.pallas_call(
        functools.partial(combine_kernel, Y),
        grid=(X,),
        out_shape=(out, out),
        in_specs=[
            pl.BlockSpec((32, 128), lambda x: (0, 0)),
            pl.BlockSpec((STEPS + 1, 1, Y, S, Z), lambda x: (0, x, 0, 0, 0)),
        ],
        out_specs=(
            pl.BlockSpec((S, 1, Y, Z), lambda x: (0, x, 0, 0)),
            pl.BlockSpec((S, 1, Y, Z), lambda x: (0, x, 0, 0)),
        ),
        scratch_shapes=[pltpu.VMEM((32, 256), jnp.bfloat16)],
        compiler_params=pltpu.CompilerParams(vmem_limit_bytes=32 * 1024 * 1024),
        name="combine",
    )(g, w)


def solution(mesh):
    placed = (P(None, "bx", "by", None), P("bx", "by", None))
    return jax.shard_map(
        shards,
        mesh=mesh,
        in_specs=placed,
        out_specs=(P(None, "bx", "by", None), P(None, "bx", "by", None)),
        check_vma=False,
    )
```

```python
import functools

import jax
import jax.numpy as jnp
import numpy as np
from jax import lax
from jax.experimental import pallas as pl
from jax.experimental.pallas import tpu as pltpu
from jax.sharding import PartitionSpec as P

S = 16
STEPS = 4
PIECES = 4
UNROLL = 2
BLOCK = 4
MESH = pl.DeviceIdType.MESH


def cheb_small():
    table = np.zeros((STEPS + 1, STEPS))
    table[0, 0] = 7.0
    table[1, 0] = 6.0
    for power in range(1, STEPS):
        table[power, power] = 7.0
        table[power - 1, power] = 3.0
        table[power + 1, power] = 3.0
    return table


def split(a):
    hi = a.astype(jnp.bfloat16)
    lo = (a - hi.astype(jnp.float32)).astype(jnp.bfloat16)
    return hi, lo


def basis_kernel(
    nbx, nby, X, Y, rhs, k_ref, w_out, g_out,
    v, kp, cx, cy, czm, czp, cd, gl, r1, r2,
    in_sem, out_sem, k_send, k_recv, h_send, h_recv, a_send, a_recv, b_send, b_recv,
):
    bx, by = lax.axis_index("bx"), lax.axis_index("by")
    barrier = pltpu.get_barrier_semaphore()

    loads = [
        pltpu.make_async_copy(rhs.at[s], v.at[0, pl.ds(1, X), pl.ds(1, Y), s], in_sem.at[s])
        for s in range(S)
    ]
    for c in loads:
        c.start()
    for d in range(1, nbx):
        pl.semaphore_signal(barrier, inc=1, device_id=(lax.rem(bx + d, nbx), by), device_id_type=MESH)
    for d in range(1, nby):
        pl.semaphore_signal(barrier, inc=1, device_id=(bx, lax.rem(by + d, nby)), device_id_type=MESH)

    @pl.loop(0, X)
    def _(x):
        kp[x + 1, pl.ds(1, Y)] = k_ref[x]

    edges = (bx > 0, bx < nbx - 1, by > 0, by < nby - 1)

    def zero_side(side):
        if side < 2:
            at = 0 if side == 0 else X + 1
            kp[at] = jnp.zeros_like(kp[at])
            for j in range(STEPS):
                @pl.loop(0, Y + 2)
                def _(y):
                    v[j, at, y] = jnp.zeros((S, 128), jnp.float32)
        else:
            at = 0 if side == 2 else Y + 1
            @pl.loop(1, X + 1)
            def _(x):
                kp[x, at] = jnp.zeros((1, 128), jnp.float32)
                for j in range(STEPS):
                    v[j, x, at] = jnp.zeros((S, 128), jnp.float32)

    for side in range(4):
        pl.when(jnp.logical_not(edges[side]))(functools.partial(zero_side, side))
    pl.semaphore_wait(barrier, nbx - 1 + nby - 1)

    YP, XP = Y // PIECES, X // PIECES

    targets = ((bx - 1, by), (bx + 1, by), (bx, by - 1), (bx, by + 1))

    def face_copies(ref, send, recv, side, piece=None):
        xs, ys = pl.ds(1, X), pl.ds(1, Y)
        if piece is not None:
            send, recv = send.at[piece], recv.at[piece]
            xs = pl.ds(1 + piece * XP, XP)
            ys = pl.ds(1 + piece * YP, YP)
        src, dst = (
            (ref.at[1, ys], ref.at[X + 1, ys]),
            (ref.at[X, ys], ref.at[0, ys]),
            (ref.at[xs, 1], ref.at[xs, Y + 1]),
            (ref.at[xs, Y], ref.at[xs, 0]),
        )[side]
        return pltpu.make_async_remote_copy(
            src_ref=src, dst_ref=dst, send_sem=send.at[side], recv_sem=recv.at[side],
            device_id=targets[side], device_id_type=MESH,
        )

    def start_faces(ref, send, recv, piece=None, sides=range(4)):
        for side in sides:
            @pl.when(edges[side])
            def _(side=side):
                face_copies(ref, send, recv, side, piece).start()

    def wait_recv(ref, send, recv, piece=None, sides=range(4)):
        for side in sides:
            @pl.when(edges[side])
            def _(side=side):
                face_copies(ref, send, recv, side ^ 1, piece).wait_recv()

    def wait_send(ref, send, recv, piece=None):
        for side in range(4):
            @pl.when(edges[side])
            def _(side=side):
                face_copies(ref, send, recv, side, piece).wait_send()

    start_faces(kp, k_send, k_recv)
    for c in loads:
        c.wait()
    for piece in [0, PIECES - 1] + list(range(1, PIECES - 1)):
        start_faces(v.at[0], h_send.at[0], h_recv.at[0], piece)
    stores = [
        pltpu.make_async_copy(
            v.at[j, pl.ds(1, X), pl.ds(1, Y)], w_out.at[j], out_sem.at[j])
        for j in range(STEPS + 1)
    ]
    stores[0].start()
    wait_recv(kp, k_send, k_recv)

    def face(a, b):
        return (2.0 * a * b) / (a + b)

    third = -1.0 / 3.0

    def coeff_x(x, n, y0):
        cx[x, pl.ds(y0, n)] = third * face(kp[x, pl.ds(y0, n)], kp[x + 1, pl.ds(y0, n)])

    @pl.loop(0, X + 1)
    def _(x):
        coeff_x(x, Y, 1)

    lane = lax.broadcasted_iota(jnp.int32, (Y, 1, 128), 2)

    @pl.loop(1, X + 1)
    def _(x):
        k = kp[x, pl.ds(1, Y)]
        cy[x, pl.ds(1, Y)] = third * face(k, kp[x, pl.ds(2, Y)])
        cy[x, pl.ds(0, 1)] = third * face(kp[x, pl.ds(0, 1)], kp[x, pl.ds(1, 1)])
        up = jnp.where(lane == 127, 0.0, pltpu.roll(k, 127, 2))
        zp = third * face(k, up)
        zm = pltpu.roll(zp, 1, 2)
        czp[x, pl.ds(1, Y)] = zp
        czm[x, pl.ds(1, Y)] = zm
        total = cx[x - 1, pl.ds(1, Y)] + cx[x, pl.ds(1, Y)]
        total = total + cy[x, pl.ds(0, Y)] + cy[x, pl.ds(1, Y)] + zp + zm
        cd[x, pl.ds(1, Y)] = -total - 2.0

    def stencil(j, x, y0, n):
        ys = pl.ds(y0, n)
        c = v[j, x, ys]
        shape = c.shape

        def wide(a):
            return jnp.broadcast_to(a, shape)

        out = wide(cd[x, ys]) * c
        out = out + wide(czp[x, ys]) * pltpu.roll(c, 127, 2)
        out = out + wide(czm[x, ys]) * pltpu.roll(c, 1, 2)
        out = out + wide(cx[x - 1, ys]) * v[j, x - 1, ys]
        out = out + wide(cx[x, ys]) * v[j, x + 1, ys]
        out = out + wide(cy[x, pl.ds(y0 - 1, n)]) * v[j, x, pl.ds(y0 - 1, n)]
        out = out + wide(cy[x, ys]) * v[j, x, pl.ds(y0 + 1, n)]
        if j == 0:
            v[1, x, ys] = 0.5 * out
        else:
            v[j + 1, x, ys] = out - v[j - 1, x, ys]

    def edge_y(j, piece):
        first = 1 if piece > 0 else 2
        last = (piece + 1) * XP + (1 if piece < PIECES - 1 else 0)

        @pl.loop(first + piece * XP, last)
        def _(x):
            stencil(j, x, 1, 1)
            stencil(j, x, Y, 1)

    def edge_x(j, piece):
        stencil(j, 1, 1 + piece * YP, YP)
        stencil(j, X, 1 + piece * YP, YP)

    def interior(j, lo, hi):
        @pl.loop(lo, hi)
        def _(x):
            stencil(j, x, 2, Y - 2)

    def flat(j, x):
        return jnp.concatenate([v[j, x, 1 + y] for y in range(Y)], axis=1)

    def gram(j, xlo, xhi, total):
        def body(x, total):
            hi, lo = split(flat(j, x))
            right = jnp.concatenate([hi, lo], axis=0)
            left = right
            if j > 0:
                phi, plo = split(flat(j - 1, x))
                left = jnp.concatenate([hi, lo, phi, plo], axis=0)
            return total + lax.dot_general(
                left, right, (((1,), (1,)), ((), ())), preferred_element_type=jnp.float32)

        n = 32 if j == 0 else 64
        if total is None:
            total = jnp.zeros((n, 32), jnp.float32)
        return lax.fori_loop(xlo, xhi, body, total, unroll=UNROLL)

    def keep(j, total):
        cols = total[:, :16] + total[:, 16:]
        same = cols[0:16] + cols[16:32]
        gl[0:16, 16 * j:16 * j + 16] = same
        if j > 0:
            gl[16:32, 16 * j:16 * j + 16] = cols[32:48] + cols[48:64]

    gl[...] = jnp.zeros_like(gl)
    order = [0, PIECES - 1] + list(range(1, PIECES - 1))
    keep(0, gram(0, 1, X + 1, None))
    for j in range(STEPS):
        ref, send, recv = v.at[j], h_send.at[j], h_recv.at[j]
        total = None
        for at, piece in enumerate(order):
            if at == 0:
                wait_recv(ref, send, recv, 0, (2, 3))
                wait_recv(ref, send, recv, PIECES - 1, (2, 3))
            elif at > 1:
                wait_recv(ref, send, recv, piece, (2, 3))
            wait_recv(ref, send, recv, piece, (0, 1))
            edge_x(j, piece)
            edge_y(j, piece)
            if j + 1 < STEPS:
                nxt = (v.at[j + 1], h_send.at[j + 1], h_recv.at[j + 1])
                start_faces(*nxt, piece, (0, 1))
                if at == 1:
                    start_faces(*nxt, 0, (2, 3))
                    start_faces(*nxt, piece, (2, 3))
                elif at > 1:
                    start_faces(*nxt, piece, (2, 3))
            lo = 1 + piece * XP
            interior(j, max(lo, 2), min(lo + XP, X))
            if j > 0:
                total = gram(j, lo, lo + XP, total)
        if j > 0:
            keep(j, total)
        stores[j + 1].start()
    keep(STEPS, gram(STEPS, 1, X + 1, None))

    def spread(axis_at, n, own, src, slots, send, recv):
        copies = []
        for d in range(1, n):
            to = (lax.rem(bx + d, n), by) if axis_at == 0 else (bx, lax.rem(by + d, n))
            copies.append(pltpu.make_async_remote_copy(
                src_ref=src, dst_ref=slots.at[d], send_sem=send.at[d], recv_sem=recv.at[d],
                device_id=to, device_id_type=MESH))
        for c in copies:
            c.start()
        total = src[...]
        for d in range(1, n):
            copies[d - 1].wait_recv()
            total = total + slots[d]
        for c in copies:
            c.wait_send()
        return total

    gl2 = r1.at[0]
    gl2[...] = spread(0, nbx, bx, gl, r1, a_send, a_recv)
    g_out[...] = spread(1, nby, by, gl2, r2, b_send, b_recv)

    wait_send(kp, k_send, k_recv)
    for j in range(STEPS):
        for piece in range(PIECES):
            wait_send(v.at[j], h_send.at[j], h_recv.at[j], piece)
    for c in stores:
        c.wait()


def solve(g):
    table = cheb_small()
    same = [g[0:16, 16 * j:16 * j + 16] for j in range(STEPS + 1)]
    cross = [None] + [g[16:32, 16 * j:16 * j + 16] for j in range(1, STEPS + 1)]
    moment = [same[0], cross[1]]
    for k in range(1, STEPS + 1):
        moment.append(2.0 * same[k] - same[0])
        if k < STEPS:
            moment.append(2.0 * cross[k + 1] - cross[1])

    def weighted(weights):
        out = None
        for m, w in zip(moment, weights):
            if w != 0.0:
                out = w * m if out is None else out + w * m
        return out

    rows = []
    for i in range(STEPS):
        blocks = []
        for j in range(STEPS):
            weights = np.zeros(2 * STEPS + 1)
            for a in range(STEPS + 1):
                for b in range(STEPS + 1):
                    w = 0.5 * table[a, i] * table[b, j]
                    weights[a + b] += w
                    weights[abs(a - b)] += w
            blocks.append(weighted([float(w) for w in weights]))
        blocks.append(weighted([float(w) for w in table[:, i]] + [0.0] * STEPS))
        blocks.append(jnp.zeros((16, 48), jnp.float32))
        rows.append(jnp.concatenate(blocks, axis=1))
    a = jnp.concatenate(rows, axis=0)
    order = S * STEPS
    place = lax.broadcasted_iota(jnp.int32, (order, 128), 0)
    for p in range(order):
        col = jnp.broadcast_to(a[:, p:p + 1], (order, 128))
        row = jnp.broadcast_to(a[p:p + 1] / col[p:p + 1], (order, 128))
        a = jnp.where(place == p, row, a - col * row)
    coeffs = [a[16 * i:16 * i + 16, order:order + 16] for i in range(STEPS)]
    zero = jnp.zeros((16, 16), jnp.float32)
    eye = jnp.where(
        lax.broadcasted_iota(jnp.int32, (16, 16), 0) == lax.broadcasted_iota(jnp.int32, (16, 16), 1),
        1.0, 0.0)
    parts = []
    for r in range(STEPS + 1):
        rest = eye if r == 0 else zero
        for i in range(STEPS):
            if table[r, i] != 0.0:
                rest = rest - float(table[r, i]) * coeffs[i]
        first = coeffs[r] if r < STEPS else zero
        parts.append(jnp.concatenate([first, rest, jnp.zeros((16, 96), jnp.float32)], axis=1))
    c = jnp.concatenate(parts, axis=0)
    hi = c.astype(jnp.bfloat16).astype(jnp.float32)
    lo = c - hi
    return jnp.concatenate([hi, hi, lo, jnp.zeros((16, 128), jnp.float32)], axis=0)


def combine_kernel(Y, g_ref, w_ref, sol_ref, res_ref, c_ref):
    @pl.when(pl.program_id(0) == 0)
    def _():
        stacked = solve(g_ref[...])
        c_ref[...] = stacked.T[0:32].astype(jnp.bfloat16)

    CH = 16

    @pl.loop(0, BLOCK * (Y // CH))
    def _(t):
        x = t // (Y // CH)
        y0 = pl.multiple_of(lax.rem(t, Y // CH) * CH, CH)
        cols = []
        for y in range(CH):
            his, los = [], []
            for j in range(STEPS + 1):
                hi, lo = split(w_ref[j, x, y0 + y])
                his.append(hi)
                los.append(lo)
            cols.append(jnp.concatenate(
                his + los + his + [jnp.zeros((16, 128), jnp.bfloat16)], axis=0))
        right = jnp.concatenate(cols, axis=1)
        out = jnp.dot(c_ref[...], right, preferred_element_type=jnp.float32)
        out = jnp.stack([out[:, 128 * y:128 * y + 128] for y in range(CH)], axis=0)
        out = jnp.swapaxes(out, 0, 1)
        sol_ref[:, x, pl.ds(y0, CH)] = out[0:16]
        res_ref[:, x, pl.ds(y0, CH)] = out[16:32]


def shards(right_side, conductivity):
    nbx, nby = lax.axis_size("bx"), lax.axis_size("by")
    X, Y, Z = conductivity.shape
    f32 = jnp.float32
    dma = pltpu.SemaphoreType.DMA
    w, g = pl.pallas_call(
        functools.partial(basis_kernel, nbx, nby, X, Y),
        out_shape=(
            jax.ShapeDtypeStruct((STEPS + 1, X, Y, S, Z), f32),
            jax.ShapeDtypeStruct((32, 128), f32),
        ),
        in_specs=[pl.BlockSpec(memory_space=pl.ANY), pl.BlockSpec(memory_space=pltpu.VMEM)],
        out_specs=(pl.BlockSpec(memory_space=pl.ANY), pl.BlockSpec(memory_space=pltpu.VMEM)),
        scratch_shapes=[
            pltpu.VMEM((STEPS + 1, X + 2, Y + 2, S, Z), f32),
            pltpu.VMEM((X + 2, Y + 2, 1, Z), f32),
            pltpu.VMEM((X + 2, Y + 2, 1, Z), f32),
            pltpu.VMEM((X + 2, Y + 2, 1, Z), f32),
            pltpu.VMEM((X + 2, Y + 2, 1, Z), f32),
            pltpu.VMEM((X + 2, Y + 2, 1, Z), f32),
            pltpu.VMEM((X + 2, Y + 2, 1, Z), f32),
            pltpu.VMEM((32, 128), f32),
            pltpu.VMEM((nbx, 32, 128), f32),
            pltpu.VMEM((nby, 32, 128), f32),
            dma((S,)), dma((STEPS + 1,)), dma((4,)), dma((4,)),
            dma((STEPS, PIECES, 4)), dma((STEPS, PIECES, 4)),
            dma((nbx,)), dma((nbx,)), dma((nby,)), dma((nby,)),
        ],
        compiler_params=pltpu.CompilerParams(
            collective_id=0, has_side_effects=True, vmem_limit_bytes=56 * 1024 * 1024),
        name="basis",
    )(right_side, conductivity.reshape(X, Y, 1, Z))
    out = jax.ShapeDtypeStruct((S, X, Y, Z), f32)
    return pl.pallas_call(
        functools.partial(combine_kernel, Y),
        grid=(X // BLOCK,),
        out_shape=(out, out),
        in_specs=[
            pl.BlockSpec((32, 128), lambda x: (0, 0)),
            pl.BlockSpec((STEPS + 1, BLOCK, Y, S, Z), lambda x: (0, x, 0, 0, 0)),
        ],
        out_specs=(
            pl.BlockSpec((S, BLOCK, Y, Z), lambda x: (0, x, 0, 0)),
            pl.BlockSpec((S, BLOCK, Y, Z), lambda x: (0, x, 0, 0)),
        ),
        scratch_shapes=[pltpu.VMEM((32, 256), jnp.bfloat16)],
        compiler_params=pltpu.CompilerParams(vmem_limit_bytes=58 * 1024 * 1024),
        name="combine",
    )(g, w)


def solution(mesh):
    placed = (P(None, "bx", "by", None), P("bx", "by", None))
    return jax.shard_map(
        shards,
        mesh=mesh,
        in_specs=placed,
        out_specs=(P(None, "bx", "by", None), P(None, "bx", "by", None)),
        check_vma=False,
    )
```

```python
import functools

import jax
import jax.numpy as jnp
import numpy as np
from jax import lax
from jax.experimental import pallas as pl
from jax.experimental.pallas import tpu as pltpu
from jax.sharding import PartitionSpec as P

S = 16
STEPS = 4
PIECES = 4
UNROLL = 2
BLOCK = 4
MESH = pl.DeviceIdType.MESH


def cheb_small():
    table = np.zeros((STEPS + 1, STEPS))
    table[0, 0] = 7.0
    table[1, 0] = 6.0
    for power in range(1, STEPS):
        table[power, power] = 7.0
        table[power - 1, power] = 3.0
        table[power + 1, power] = 3.0
    return table


def split(a):
    hi = a.astype(jnp.bfloat16)
    lo = (a - hi.astype(jnp.float32)).astype(jnp.bfloat16)
    return hi, lo


def basis_kernel(
    nbx, nby, X, Y, rhs, k_ref, w_out, g_out,
    v, kp, cx, cy, czm, czp, cd, gl, r1, r2,
    in_sem, out_sem, k_send, k_recv, h_send, h_recv, a_send, a_recv, b_send, b_recv,
):
    bx, by = lax.axis_index("bx"), lax.axis_index("by")
    barrier = pltpu.get_barrier_semaphore()

    loads = [
        pltpu.make_async_copy(rhs.at[s], v.at[0, pl.ds(1, X), pl.ds(1, Y), s], in_sem.at[s])
        for s in range(S)
    ]
    for c in loads:
        c.start()
    for d in range(1, nbx):
        pl.semaphore_signal(barrier, inc=1, device_id=(lax.rem(bx + d, nbx), by), device_id_type=MESH)
    for d in range(1, nby):
        pl.semaphore_signal(barrier, inc=1, device_id=(bx, lax.rem(by + d, nby)), device_id_type=MESH)

    @pl.loop(0, X)
    def _(x):
        kp[x + 1, pl.ds(1, Y)] = k_ref[x]

    edges = (bx > 0, bx < nbx - 1, by > 0, by < nby - 1)

    def zero_side(side):
        if side < 2:
            at = 0 if side == 0 else X + 1
            kp[at] = jnp.zeros_like(kp[at])
            for j in range(STEPS):
                @pl.loop(0, Y + 2)
                def _(y):
                    v[j, at, y] = jnp.zeros((S, 128), jnp.float32)
        else:
            at = 0 if side == 2 else Y + 1
            @pl.loop(1, X + 1)
            def _(x):
                kp[x, at] = jnp.zeros((1, 128), jnp.float32)
                for j in range(STEPS):
                    v[j, x, at] = jnp.zeros((S, 128), jnp.float32)

    for side in range(4):
        pl.when(jnp.logical_not(edges[side]))(functools.partial(zero_side, side))
    pl.semaphore_wait(barrier, nbx - 1 + nby - 1)

    YP, XP = Y // PIECES, X // PIECES

    targets = ((bx - 1, by), (bx + 1, by), (bx, by - 1), (bx, by + 1))

    def face_copies(ref, send, recv, side, piece=None):
        xs, ys = pl.ds(1, X), pl.ds(1, Y)
        if piece is not None:
            send, recv = send.at[piece], recv.at[piece]
            xs = pl.ds(1 + piece * XP, XP)
            ys = pl.ds(1 + piece * YP, YP)
        src, dst = (
            (ref.at[1, ys], ref.at[X + 1, ys]),
            (ref.at[X, ys], ref.at[0, ys]),
            (ref.at[xs, 1], ref.at[xs, Y + 1]),
            (ref.at[xs, Y], ref.at[xs, 0]),
        )[side]
        return pltpu.make_async_remote_copy(
            src_ref=src, dst_ref=dst, send_sem=send.at[side], recv_sem=recv.at[side],
            device_id=targets[side], device_id_type=MESH,
        )

    def start_faces(ref, send, recv, piece=None, sides=range(4)):
        for side in sides:
            @pl.when(edges[side])
            def _(side=side):
                face_copies(ref, send, recv, side, piece).start()

    def wait_recv(ref, send, recv, piece=None, sides=range(4)):
        for side in sides:
            @pl.when(edges[side])
            def _(side=side):
                face_copies(ref, send, recv, side ^ 1, piece).wait_recv()

    def wait_send(ref, send, recv, piece=None):
        for side in range(4):
            @pl.when(edges[side])
            def _(side=side):
                face_copies(ref, send, recv, side, piece).wait_send()

    start_faces(kp, k_send, k_recv)
    for c in loads:
        c.wait()
    for piece in [0, PIECES - 1] + list(range(1, PIECES - 1)):
        start_faces(v.at[0], h_send.at[0], h_recv.at[0], piece)
    stores = [
        pltpu.make_async_copy(
            v.at[j, pl.ds(1, X), pl.ds(1, Y)], w_out.at[j], out_sem.at[j])
        for j in range(STEPS + 1)
    ]
    stores[0].start()
    wait_recv(kp, k_send, k_recv)

    def face(a, b):
        return (2.0 * a * b) / (a + b)

    third = -1.0 / 3.0

    def coeff_x(x, n, y0):
        cx[x, pl.ds(y0, n)] = third * face(kp[x, pl.ds(y0, n)], kp[x + 1, pl.ds(y0, n)])

    @pl.loop(0, X + 1)
    def _(x):
        coeff_x(x, Y, 1)

    lane = lax.broadcasted_iota(jnp.int32, (Y, 1, 128), 2)

    @pl.loop(1, X + 1)
    def _(x):
        k = kp[x, pl.ds(1, Y)]
        cy[x, pl.ds(1, Y)] = third * face(k, kp[x, pl.ds(2, Y)])
        cy[x, pl.ds(0, 1)] = third * face(kp[x, pl.ds(0, 1)], kp[x, pl.ds(1, 1)])
        up = jnp.where(lane == 127, 0.0, pltpu.roll(k, 127, 2))
        zp = third * face(k, up)
        zm = pltpu.roll(zp, 1, 2)
        czp[x, pl.ds(1, Y)] = zp
        czm[x, pl.ds(1, Y)] = zm
        total = cx[x - 1, pl.ds(1, Y)] + cx[x, pl.ds(1, Y)]
        total = total + cy[x, pl.ds(0, Y)] + cy[x, pl.ds(1, Y)] + zp + zm
        cd[x, pl.ds(1, Y)] = -total - 2.0

    def stencil(j, x, y0, n):
        ys = pl.ds(y0, n)
        c = v[j, x, ys]
        shape = c.shape

        def wide(a):
            return jnp.broadcast_to(a, shape)

        out = wide(cd[x, ys]) * c
        out = out + wide(czp[x, ys]) * pltpu.roll(c, 127, 2)
        out = out + wide(czm[x, ys]) * pltpu.roll(c, 1, 2)
        out = out + wide(cx[x - 1, ys]) * v[j, x - 1, ys]
        out = out + wide(cx[x, ys]) * v[j, x + 1, ys]
        out = out + wide(cy[x, pl.ds(y0 - 1, n)]) * v[j, x, pl.ds(y0 - 1, n)]
        out = out + wide(cy[x, ys]) * v[j, x, pl.ds(y0 + 1, n)]
        if j == 0:
            v[1, x, ys] = 0.5 * out
        else:
            v[j + 1, x, ys] = out - v[j - 1, x, ys]

    def edge_y(j, piece):
        first = 1 if piece > 0 else 2
        last = (piece + 1) * XP + (1 if piece < PIECES - 1 else 0)

        @pl.loop(first + piece * XP, last)
        def _(x):
            stencil(j, x, 1, 1)
            stencil(j, x, Y, 1)

    def edge_x(j, piece):
        stencil(j, 1, 1 + piece * YP, YP)
        stencil(j, X, 1 + piece * YP, YP)

    def interior(j, lo, hi):
        @pl.loop(lo, hi)
        def _(x):
            stencil(j, x, 2, Y - 2)

    def flat(j, x):
        return jnp.concatenate([v[j, x, 1 + y] for y in range(Y)], axis=1)

    def gram(j, xlo, xhi, total):
        def body(x, total):
            hi, lo = split(flat(j, x))
            right = jnp.concatenate([hi, lo], axis=0)
            left = right
            if j > 0:
                phi, plo = split(flat(j - 1, x))
                left = jnp.concatenate([hi, lo, phi, plo], axis=0)
            return total + lax.dot_general(
                left, right, (((1,), (1,)), ((), ())), preferred_element_type=jnp.float32)

        n = 32 if j == 0 else 64
        if total is None:
            total = jnp.zeros((n, 32), jnp.float32)
        return lax.fori_loop(xlo, xhi, body, total, unroll=UNROLL)

    def keep(j, total):
        cols = total[:, :16] + total[:, 16:]
        same = cols[0:16] + cols[16:32]
        gl[0:16, 16 * j:16 * j + 16] = same
        if j > 0:
            gl[16:32, 16 * j:16 * j + 16] = cols[32:48] + cols[48:64]

    gl[...] = jnp.zeros_like(gl)
    order = [0, PIECES - 1] + list(range(1, PIECES - 1))
    keep(0, gram(0, 1, X + 1, None))
    for j in range(STEPS):
        ref, send, recv = v.at[j], h_send.at[j], h_recv.at[j]
        total = None
        for at, piece in enumerate(order):
            if at == 0:
                wait_recv(ref, send, recv, 0, (2, 3))
                wait_recv(ref, send, recv, PIECES - 1, (2, 3))
            elif at > 1:
                wait_recv(ref, send, recv, piece, (2, 3))
            wait_recv(ref, send, recv, piece, (0, 1))
            edge_x(j, piece)
            edge_y(j, piece)
            if j + 1 < STEPS:
                nxt = (v.at[j + 1], h_send.at[j + 1], h_recv.at[j + 1])
                start_faces(*nxt, piece, (0, 1))
                if at == 1:
                    start_faces(*nxt, 0, (2, 3))
                    start_faces(*nxt, piece, (2, 3))
                elif at > 1:
                    start_faces(*nxt, piece, (2, 3))
            lo = 1 + piece * XP
            interior(j, max(lo, 2), min(lo + XP, X))
            if j > 0:
                total = gram(j, lo, lo + XP, total)
        if j > 0:
            keep(j, total)
        stores[j + 1].start()
    keep(STEPS, gram(STEPS, 1, X + 1, None))

    def spread(axis_at, n, own, src, slots, send, recv):
        copies = []
        for d in range(1, n):
            to = (lax.rem(bx + d, n), by) if axis_at == 0 else (bx, lax.rem(by + d, n))
            copies.append(pltpu.make_async_remote_copy(
                src_ref=src, dst_ref=slots.at[d], send_sem=send.at[d], recv_sem=recv.at[d],
                device_id=to, device_id_type=MESH))
        for c in copies:
            c.start()
        total = src[...]
        for d in range(1, n):
            copies[d - 1].wait_recv()
            total = total + slots[d]
        for c in copies:
            c.wait_send()
        return total

    gl2 = r1.at[0]
    gl2[...] = spread(0, nbx, bx, gl, r1, a_send, a_recv)
    g_out[...] = spread(1, nby, by, gl2, r2, b_send, b_recv)

    wait_send(kp, k_send, k_recv)
    for j in range(STEPS):
        for piece in range(PIECES):
            wait_send(v.at[j], h_send.at[j], h_recv.at[j], piece)
    for c in stores:
        c.wait()


def solve(g):
    table = cheb_small()
    same = [g[0:16, 16 * j:16 * j + 16] for j in range(STEPS + 1)]
    cross = [None] + [g[16:32, 16 * j:16 * j + 16] for j in range(1, STEPS + 1)]
    moment = [same[0], cross[1]]
    for k in range(1, STEPS + 1):
        moment.append(2.0 * same[k] - same[0])
        if k < STEPS:
            moment.append(2.0 * cross[k + 1] - cross[1])

    def weighted(weights):
        out = None
        for m, w in zip(moment, weights):
            if w != 0.0:
                out = w * m if out is None else out + w * m
        return out

    rows = []
    for i in range(STEPS):
        blocks = []
        for j in range(STEPS):
            weights = np.zeros(2 * STEPS + 1)
            for a in range(STEPS + 1):
                for b in range(STEPS + 1):
                    w = 0.5 * table[a, i] * table[b, j]
                    weights[a + b] += w
                    weights[abs(a - b)] += w
            blocks.append(weighted([float(w) for w in weights]))
        blocks.append(weighted([float(w) for w in table[:, i]] + [0.0] * STEPS))
        blocks.append(jnp.zeros((16, 48), jnp.float32))
        rows.append(jnp.concatenate(blocks, axis=1))
    a = jnp.concatenate(rows, axis=0)
    order = S * STEPS
    place = lax.broadcasted_iota(jnp.int32, (order, 128), 0)
    for p in range(0, order, 2):
        one = jnp.broadcast_to(a[:, p:p + 1], (order, 128))
        two = jnp.broadcast_to(a[:, p + 1:p + 2], (order, 128))
        inverse = 1.0 / one[p:p + 1]
        first = a[p:p + 1] * inverse
        low = one[p + 1:p + 2]
        high = two[p:p + 1] * inverse
        second = (a[p + 1:p + 2] - low * first) / (two[p + 1:p + 2] - low * high)
        first = first - high * second
        rest = a - one * first - two * second
        a = jnp.where(place == p, first, jnp.where(place == p + 1, second, rest))
    coeffs = [a[16 * i:16 * i + 16, order:order + 16] for i in range(STEPS)]
    zero = jnp.zeros((16, 16), jnp.float32)
    eye = jnp.where(
        lax.broadcasted_iota(jnp.int32, (16, 16), 0) == lax.broadcasted_iota(jnp.int32, (16, 16), 1),
        1.0, 0.0)
    parts = []
    for r in range(STEPS + 1):
        rest = eye if r == 0 else zero
        for i in range(STEPS):
            if table[r, i] != 0.0:
                rest = rest - float(table[r, i]) * coeffs[i]
        first = coeffs[r] if r < STEPS else zero
        parts.append(jnp.concatenate([first, rest, jnp.zeros((16, 96), jnp.float32)], axis=1))
    c = jnp.concatenate(parts, axis=0)
    hi = c.astype(jnp.bfloat16).astype(jnp.float32)
    lo = c - hi
    return jnp.concatenate([hi, hi, lo, jnp.zeros((16, 128), jnp.float32)], axis=0)


def combine_kernel(Y, g_ref, w_ref, sol_ref, res_ref, c_ref):
    @pl.when(pl.program_id(0) == 0)
    def _():
        stacked = solve(g_ref[...])
        c_ref[...] = stacked.T[0:32].astype(jnp.bfloat16)

    CH = 16

    @pl.loop(0, BLOCK * (Y // CH))
    def _(t):
        x = t // (Y // CH)
        y0 = pl.multiple_of(lax.rem(t, Y // CH) * CH, CH)
        cols = []
        for y in range(CH):
            his, los = [], []
            for j in range(STEPS + 1):
                hi, lo = split(w_ref[j, x, y0 + y])
                his.append(hi)
                los.append(lo)
            cols.append(jnp.concatenate(
                his + los + his + [jnp.zeros((16, 128), jnp.bfloat16)], axis=0))
        right = jnp.concatenate(cols, axis=1)
        out = jnp.dot(c_ref[...], right, preferred_element_type=jnp.float32)
        out = jnp.stack([out[:, 128 * y:128 * y + 128] for y in range(CH)], axis=0)
        out = jnp.swapaxes(out, 0, 1)
        sol_ref[:, x, pl.ds(y0, CH)] = out[0:16]
        res_ref[:, x, pl.ds(y0, CH)] = out[16:32]


def shards(right_side, conductivity):
    nbx, nby = lax.axis_size("bx"), lax.axis_size("by")
    X, Y, Z = conductivity.shape
    f32 = jnp.float32
    dma = pltpu.SemaphoreType.DMA
    w, g = pl.pallas_call(
        functools.partial(basis_kernel, nbx, nby, X, Y),
        out_shape=(
            jax.ShapeDtypeStruct((STEPS + 1, X, Y, S, Z), f32),
            jax.ShapeDtypeStruct((32, 128), f32),
        ),
        in_specs=[pl.BlockSpec(memory_space=pl.ANY), pl.BlockSpec(memory_space=pltpu.VMEM)],
        out_specs=(pl.BlockSpec(memory_space=pl.ANY), pl.BlockSpec(memory_space=pltpu.VMEM)),
        scratch_shapes=[
            pltpu.VMEM((STEPS + 1, X + 2, Y + 2, S, Z), f32),
            pltpu.VMEM((X + 2, Y + 2, 1, Z), f32),
            pltpu.VMEM((X + 2, Y + 2, 1, Z), f32),
            pltpu.VMEM((X + 2, Y + 2, 1, Z), f32),
            pltpu.VMEM((X + 2, Y + 2, 1, Z), f32),
            pltpu.VMEM((X + 2, Y + 2, 1, Z), f32),
            pltpu.VMEM((X + 2, Y + 2, 1, Z), f32),
            pltpu.VMEM((32, 128), f32),
            pltpu.VMEM((nbx, 32, 128), f32),
            pltpu.VMEM((nby, 32, 128), f32),
            dma((S,)), dma((STEPS + 1,)), dma((4,)), dma((4,)),
            dma((STEPS, PIECES, 4)), dma((STEPS, PIECES, 4)),
            dma((nbx,)), dma((nbx,)), dma((nby,)), dma((nby,)),
        ],
        compiler_params=pltpu.CompilerParams(
            collective_id=0, has_side_effects=True, vmem_limit_bytes=56 * 1024 * 1024),
        name="basis",
    )(right_side, conductivity.reshape(X, Y, 1, Z))
    out = jax.ShapeDtypeStruct((S, X, Y, Z), f32)
    return pl.pallas_call(
        functools.partial(combine_kernel, Y),
        grid=(X // BLOCK,),
        out_shape=(out, out),
        in_specs=[
            pl.BlockSpec((32, 128), lambda x: (0, 0)),
            pl.BlockSpec((STEPS + 1, BLOCK, Y, S, Z), lambda x: (0, x, 0, 0, 0)),
        ],
        out_specs=(
            pl.BlockSpec((S, BLOCK, Y, Z), lambda x: (0, x, 0, 0)),
            pl.BlockSpec((S, BLOCK, Y, Z), lambda x: (0, x, 0, 0)),
        ),
        scratch_shapes=[pltpu.VMEM((32, 256), jnp.bfloat16)],
        compiler_params=pltpu.CompilerParams(vmem_limit_bytes=58 * 1024 * 1024),
        name="combine",
    )(g, w)


def solution(mesh):
    placed = (P(None, "bx", "by", None), P("bx", "by", None))
    return jax.shard_map(
        shards,
        mesh=mesh,
        in_specs=placed,
        out_specs=(P(None, "bx", "by", None), P(None, "bx", "by", None)),
        check_vma=False,
    )
```
